1024 devices in a mesh: section: 16 (over y, z_lo), dp: 8 (over z_hi, core), tensor: 8 (over x).
Axes of the slice: x: 8, y: 8, z: 8 (z_hi: 4, z_lo: 2; z = z_hi * 2 + z_lo), core: 2. Of those that a mesh axis runs over, the one named last changes fastest.
Arguments:
- down_hidden: bfloat16 [16, 512, 4096], P('section', 'dp'), may hold values from -6 to 6
- up_hidden: bfloat16 [16, 512, 4096], P('section', 'dp'), may hold values from -6 to 6
- down_cot: bfloat16 [16, 512, 1024], P('section', 'dp', 'tensor'), may hold values from -0.19921875 to 0.19921875
- up_cot: bfloat16 [16, 512, 1024], P('section', 'dp', 'tensor'), may hold values from -0.19921875 to 0.19921875
- down_weight: bfloat16 [16, 4096, 1024], P('section', None, 'tensor'), may hold values from -0.09375 to 0.09375
- up_weight: bfloat16 [16, 4096, 1024], P('section', None, 'tensor'), may hold values from -0.09375 to 0.09375
- master: float32 [16, 2, 4096, 1024], P('section', None, 'dp', 'tensor'), may hold values from -3 to 3
- moment1: float32 [16, 2, 4096, 1024], P('section', None, 'dp', 'tensor'), may hold values from -1.2 to 1.2
- moment2: float32 [16, 2, 4096, 1024], P('section', None, 'dp', 'tensor'), may hold values from 0.01 to 1
Outputs:
- down_values: bfloat16 [16, 512, 1024], P('section', 'dp', 'tensor')
- up_values: bfloat16 [16, 512, 1024], P('section', 'dp', 'tensor')
- new_master: float32 [16, 2, 4096, 1024], P('section', None, 'dp', 'tensor')
- new_moment1: float32 [16, 2, 4096, 1024], P('section', None, 'dp', 'tensor')
- new_moment2: float32 [16, 2, 4096, 1024], P('section', None, 'dp', 'tensor')
The draws below stay inside these ranges and needn't reach their ends.
All inputs are finite; a program needn't handle non-finite values.
Results may differ from the reference program's by a relative error of at most 0.0075.
Values may be sent and summed in bfloat16 or wider, within the bound.
A program may use at most 32 MiB of HBM per device.

```python
import math
import jax
import jax.numpy as jnp
from jax import lax

D = 4096
STEP = 20
SECTIONS = 16
KVW = 1024
TOKENS = 512


def shard_levels(own_key, dims, cuts, smallest, top_value):
    gain, own = 1.0, jax.random.fold_in(own_key, 6)
    for dim, blocks in cuts:
        steps = jnp.exp(jax.random.uniform(jax.random.fold_in(own, dim), (blocks,), jnp.float32, smallest / len(cuts), top_value / len(cuts)))
        gain = gain * jnp.repeat(steps, dims[dim] // blocks).reshape([-1 if axis == dim else 1 for axis in range(len(dims))])
    return gain


def centred(key, dims, scale, reach, cuts=(), held_as=jnp.bfloat16):
    array = jax.random.normal(key, dims, jnp.float32) * scale
    if len(cuts) > 0:
        array = shard_levels(key, dims, cuts, -0.22, 0.18) * array
    return jnp.clip(array, min=-reach, max=reach).astype(held_as)


def setup_inputs(seed: int = 0) -> dict:
    seeds = jax.random.split(jax.random.key(seed), 10)
    down_hidden = centred(seeds[0], (SECTIONS, TOKENS, D), 1.0, 6.0, ((0, 16), (1, 8)))
    up_hidden = centred(seeds[1], (SECTIONS, TOKENS, D), 1.0, 6.0, ((0, 16), (1, 8)))
    down_cot = centred(seeds[2], (SECTIONS, TOKENS, KVW), 0.03, 0.19921875, ((0, 16), (1, 8), (2, 8)))
    up_cot = centred(seeds[3], (SECTIONS, TOKENS, KVW), 0.03, 0.19921875, ((0, 16), (1, 8), (2, 8)))
    down_weight = centred(seeds[4], (SECTIONS, D, KVW), D ** -0.5, 0.09375, ((0, 16), (2, 8)))
    up_weight = centred(seeds[5], (SECTIONS, D, KVW), D ** -0.5, 0.09375, ((0, 16), (2, 8)))
    master = centred(seeds[6], (SECTIONS, 2, D, KVW), 0.5, 3.0, ((0, 16), (2, 8), (3, 8)), jnp.float32)
    moment1 = centred(seeds[7], (SECTIONS, 2, D, KVW), 0.2, 1.2, ((0, 16), (2, 8), (3, 8)), jnp.float32)
    moment2 = jnp.clip(jnp.exp(math.log(1.0) - 4.6051702 * jax.random.uniform(seeds[8], (SECTIONS, 2, D, KVW), jnp.float32) ** shard_levels(seeds[8], (SECTIONS, 2, D, KVW), ((0, 16), (2, 8), (3, 8)), -0.2, 0.2)), 0.01, 1.0)
    return {"down_hidden": down_hidden, "up_hidden": up_hidden, "down_cot": down_cot, "up_cot": up_cot, "down_weight": down_weight, "up_weight": up_weight, "master": master, "moment1": moment1, "moment2": moment2}


def normalize(hidden):
    values = hidden.astype(jnp.float32)
    factor = lax.rsqrt(lax.optimization_barrier(jnp.mean(values * values, axis=-1, keepdims=True)) + 1e-05)
    return (values * factor).astype(jnp.bfloat16)

def reference(down_hidden, up_hidden, down_cot, up_cot, down_weight, up_weight, master, moment1, moment2):
    down_normed = normalize(jnp.roll(down_hidden, 1, axis=0))
    up_normed = normalize(jnp.roll(up_hidden, -1, axis=0))
    down_values = jnp.einsum('std,sdc->stc', down_normed.astype(jnp.float32), down_weight.astype(jnp.float32)).astype(jnp.bfloat16)
    up_values = jnp.einsum('std,sdc->stc', up_normed.astype(jnp.float32), up_weight.astype(jnp.float32)).astype(jnp.bfloat16)
    grad_down = jnp.einsum('std,stc->sdc', down_normed.astype(jnp.float32), down_cot.astype(jnp.float32))
    grad_up = jnp.einsum('std,stc->sdc', up_normed.astype(jnp.float32), up_cot.astype(jnp.float32))
    totals = jnp.stack([grad_down + grad_up[::-1], grad_up + grad_down[::-1]], axis=1)
    new_moment1 = 0.9 * moment1 + 0.1 * totals
    new_moment2 = 0.95 * moment2 + 0.05 * totals * totals
    first_fix = 1.0 - 0.9 ** STEP
    second_fix = 1.0 - 0.95 ** STEP
    new_master = master - 0.05 * (new_moment1 / first_fix) / (jnp.sqrt(new_moment2 / second_fix) + 1e-08)
    return (down_values, up_values, new_master, new_moment1, new_moment2)
```

```python
import functools
import jax
import jax.numpy as jnp
from jax import lax
from jax.experimental import pallas as pl
from jax.experimental.pallas import tpu as pltpu
from jax.sharding import PartitionSpec as P

STEP = 20
MESH = pl.DeviceIdType.MESH


def relay_kernel(
    down_hidden, up_hidden, down_cot, up_cot, down_weight, up_weight,
    totals, down_values, up_values,
    raw, normed, feats, cots, weights, grad_out, grad_in, part_out, part_in,
    load_sem, relay_send, relay_recv, cot_send, cot_recv, ring_send, right_recv, left_recv,
    part_send, part_recv, grad_send, grad_recv,
):
    sections, dp, tensor = (lax.axis_size(a) for a in ("section", "dp", "tensor"))
    s, d, t = (lax.axis_index(a) for a in ("section", "dp", "tensor"))
    rows = raw.shape[1]
    blocks = feats.shape[2]
    onward = (lax.rem(s + 1, sections), lax.rem(s + sections - 1, sections))
    right, left = lax.rem(t + 1, tensor), lax.rem(t + tensor - 1, tensor)
    mirror = sections - 1 - s
    group, half = lax.div(t, 2), lax.rem(t, 2)

    loads = []
    for way, source in enumerate((down_hidden, up_hidden)):
        loads.append(pltpu.make_async_copy(source.at[group], raw.at[way], load_sem.at[way]))
    for way, source in enumerate((down_cot, up_cot)):
        loads.append(pltpu.make_async_copy(source, cots.at[d, way], load_sem.at[2 + way]))
    for way, source in enumerate((down_weight, up_weight)):
        loads.append(pltpu.make_async_copy(source.at[d], weights.at[way], load_sem.at[4 + way]))
    for load in loads:
        load.start()

    barrier = pltpu.get_barrier_semaphore()
    for peer in range(dp):
        for way in range(2):
            pl.semaphore_signal(barrier, device_id={"section": onward[way], "dp": peer}, device_id_type=MESH)
    for step in range(1, dp):
        pl.semaphore_signal(barrier, device_id={"dp": lax.rem(d + step, dp)}, device_id_type=MESH)
    pl.semaphore_signal(barrier, device_id={"tensor": right}, device_id_type=MESH)
    pl.semaphore_signal(barrier, device_id={"tensor": left}, device_id_type=MESH)
    pl.semaphore_signal(barrier, device_id={"section": mirror}, device_id_type=MESH)

    for way in range(2):
        loads[way].wait()
        values = raw[way].astype(jnp.float32)
        factor = lax.rsqrt(jnp.mean(values * values, axis=-1, keepdims=True) + 1e-05)
        scaled = (values * factor).astype(jnp.bfloat16)
        for block in range(normed.shape[1]):
            normed[way, block] = scaled[:, block * 128 : (block + 1) * 128]
    pl.semaphore_wait(barrier, 2 * dp + dp - 1 + 3)

    for way in range(2):
        for peer in range(dp):
            pltpu.make_async_remote_copy(
                src_ref=normed.at[way, pl.ds((peer * 2 + half) * blocks, blocks)],
                dst_ref=feats.at[way, t, :, d],
                send_sem=relay_send,
                recv_sem=relay_recv.at[way],
                device_id={"section": onward[way], "dp": peer},
                device_id_type=MESH,
            ).start()
    loads[2].wait()
    loads[3].wait()
    for step in range(1, dp):
        pltpu.make_async_remote_copy(
            src_ref=cots.at[d],
            dst_ref=cots.at[d],
            send_sem=cot_send,
            recv_sem=cot_recv,
            device_id={"dp": lax.rem(d + step, dp)},
            device_id_type=MESH,
        ).start()
    loads[4].wait()
    loads[5].wait()

    half_ring = tensor // 2
    hops = ((half_ring, tensor - 1 - half_ring), (tensor - 1 - half_ring, half_ring))

    def send_on(way, block, step, rightward):
        origin = lax.rem(t + tensor - step, tensor) if rightward else lax.rem(t + step, tensor)
        recv = right_recv if rightward else left_recv
        piece = feats.at[way, origin, block]
        return pltpu.make_async_remote_copy(
            src_ref=piece,
            dst_ref=piece,
            send_sem=ring_send,
            recv_sem=recv.at[way, block, step],
            device_id={"tensor": right if rightward else left},
            device_id_type=MESH,
        )

    def arrived(way, block, step, rightward):
        origin = lax.rem(t + 2 * tensor - step - 1, tensor) if rightward else lax.rem(t + step + 1, tensor)
        recv = right_recv if rightward else left_recv
        piece = feats.at[way, origin, block]
        pltpu.make_async_copy(piece, piece, recv.at[way, block, step]).wait()

    def gradient(way, block):
        features = jnp.concatenate(
            [
                jnp.concatenate([feats[way, 2 * g + h, block].reshape(-1, 128) for g in range(tensor // 2)], axis=0)
                for h in range(2)
            ],
            axis=1,
        )
        cot = jnp.concatenate([cots[:, way, g].reshape(-1, 128) for g in range(tensor // 2)], axis=0)
        grad = lax.dot_general(features, cot, (((0,), (0,)), ((), ())), preferred_element_type=jnp.float32)
        grad = grad.reshape(2, 128, 128)
        totals[way, :, block] = grad
        grad_out[way, block] = grad.astype(jnp.bfloat16)
        mirrored(way, block).start()

    def mirrored(way, block):
        return pltpu.make_async_remote_copy(
            src_ref=grad_out.at[way, block],
            dst_ref=grad_in.at[way, block],
            send_sem=grad_send.at[way, block],
            recv_sem=grad_recv.at[way, block],
            device_id={"section": mirror},
            device_id_type=MESH,
        )

    def project(way):
        for g in range(tensor // 2):
            features = jnp.concatenate(
                [feats[way, 2 * g + h, block].reshape(-1, 128) for h in range(2) for block in range(blocks)], axis=1
            )
            part = jnp.dot(features, weights[way], preferred_element_type=jnp.float32)
            part_out[way, :, g] = part.astype(jnp.bfloat16).reshape(dp, rows, 128)
        for step in range(1, dp):
            peer = lax.rem(d + step, dp)
            pltpu.make_async_remote_copy(
                src_ref=part_out.at[way, peer],
                dst_ref=part_in.at[way, step - 1],
                send_sem=part_send,
                recv_sem=part_recv.at[way],
                device_id={"dp": peer},
                device_id_type=MESH,
            ).start()

    stages = [(way, block) for way in range(2) for block in range(blocks)]
    events = []
    for index, (way, block) in enumerate(stages):
        for step in range(half_ring + 1):
            events.append((index + step, step, index))
    for _, step, index in sorted(events, key=lambda e: (e[0], -e[1])):
        way, block = stages[index]
        if step == 0:
            if block == 0:
                pltpu.make_async_copy(feats.at[way, t], feats.at[way, t], relay_recv.at[way]).wait()
        for rightward in (True, False):
            limit = hops[way][0 if rightward else 1]
            if 1 <= step <= limit:
                arrived(way, block, step - 1, rightward)
            if step < limit:
                send_on(way, block, step, rightward).start()
        if step == half_ring:
            if index == 0:
                pltpu.make_async_copy(cots.at[pl.ds(0, dp - 1)], cots.at[pl.ds(0, dp - 1)], cot_recv).wait()
            gradient(way, block)
            if block == blocks - 1:
                project(way)

    for way in range(2):
        for block in range(blocks):
            mirrored(way, block).wait_recv()
            totals[1 - way, :, block] += grad_in[way, block].astype(jnp.float32)
        pltpu.make_async_copy(part_in.at[way], part_in.at[way], part_recv.at[way]).wait()
        total = part_out[way, d].astype(jnp.float32)
        for step in range(dp - 1):
            total += part_in[way, step].astype(jnp.float32)
        (down_values, up_values)[way][...] = total.astype(jnp.bfloat16)

    sent = normed.at[:, pl.ds(0, dp * blocks)]
    pltpu.make_async_copy(sent, sent, relay_send).wait()
    pltpu.make_async_copy(cots.at[pl.ds(0, dp - 1)], cots.at[pl.ds(0, dp - 1)], cot_send).wait()
    sent = feats.at[:, pl.ds(0, tensor - 1)]
    pltpu.make_async_copy(sent, sent, ring_send).wait()
    pltpu.make_async_copy(part_in, part_in, part_send).wait()
    for way in range(2):
        for block in range(blocks):
            mirrored(way, block).wait_send()


def shards(
    down_hidden, up_hidden, down_cot, up_cot, down_weight, up_weight, master, moment1, moment2
):
    sections, dp, tensor = (lax.axis_size(a) for a in ("section", "dp", "tensor"))
    tokens, width = down_hidden.shape[1:]
    groups = tensor // 2
    rows = tokens // groups
    shard = width // dp
    blocks = shard // 2 // 128
    hbm = pl.BlockSpec(memory_space=pltpu.HBM)
    vmem = pl.BlockSpec(memory_space=pltpu.VMEM)
    bf16, f32 = jnp.bfloat16, jnp.float32
    DMA = pltpu.SemaphoreType.DMA
    totals, down_values, up_values = pl.pallas_call(
        relay_kernel,
        out_shape=(
            jax.ShapeDtypeStruct((2, 2, blocks, 128, 128), f32),
            jax.ShapeDtypeStruct((groups, rows, 128), bf16),
            jax.ShapeDtypeStruct((groups, rows, 128), bf16),
        ),
        in_specs=[hbm] * 6,
        out_specs=(vmem, vmem, vmem),
        scratch_shapes=[
            pltpu.VMEM((2, rows, width), bf16),
            pltpu.VMEM((2, width // 128, rows, 128), bf16),
            pltpu.VMEM((2, tensor, blocks, dp, rows, 128), bf16),
            pltpu.VMEM((dp, 2, groups, rows, 128), bf16),
            pltpu.VMEM((2, shard, 128), bf16),
            pltpu.VMEM((2, blocks, 2, 128, 128), bf16),
            pltpu.VMEM((2, blocks, 2, 128, 128), bf16),
            pltpu.VMEM((2, dp, groups, rows, 128), bf16),
            pltpu.VMEM((2, dp - 1, groups, rows, 128), bf16),
            DMA((6,)),
            DMA,
            DMA((2,)),
            DMA,
            DMA,
            DMA,
            DMA((2, blocks, tensor // 2)),
            DMA((2, blocks, tensor // 2)),
            DMA,
            DMA((2,)),
            DMA((2, blocks)),
            DMA((2, blocks)),
        ],
        compiler_params=pltpu.CompilerParams(
            collective_id=0, has_side_effects=True, vmem_limit_bytes=60 * 1024 * 1024
        ),
    )(
        down_hidden.reshape(groups, rows, width),
        up_hidden.reshape(groups, rows, width),
        down_cot.reshape(groups, rows, 128),
        up_cot.reshape(groups, rows, 128),
        down_weight.reshape(dp, shard, 128),
        up_weight.reshape(dp, shard, 128),
    )
    totals = totals.reshape(master.shape)
    new_moment1 = 0.9 * moment1 + 0.1 * totals
    new_moment2 = 0.95 * moment2 + 0.05 * totals * totals
    first_fix = 1.0 - 0.9**STEP
    second_fix = 1.0 - 0.95**STEP
    new_master = master - 0.05 * (new_moment1 / first_fix) / (
        jnp.sqrt(new_moment2 / second_fix) + 1e-08
    )
    return (
        down_values.reshape(down_cot.shape),
        up_values.reshape(up_cot.shape),
        new_master,
        new_moment1,
        new_moment2,
    )


def solution(mesh):
    return jax.shard_map(
        shards,
        mesh=mesh,
        in_specs=(
            P("section", "dp", None),
            P("section", "dp", None),
            P("section", "dp", "tensor"),
            P("section", "dp", "tensor"),
            P("section", None, "tensor"),
            P("section", None, "tensor"),
            P("section", None, "dp", "tensor"),
            P("section", None, "dp", "tensor"),
            P("section", None, "dp", "tensor"),
        ),
        out_specs=(
            P("section", "dp", "tensor"),
            P("section", "dp", "tensor"),
            P("section", None, "dp", "tensor"),
            P("section", None, "dp", "tensor"),
            P("section", None, "dp", "tensor"),
        ),
        check_vma=False,
    )
```

```python
import functools
import jax
import jax.numpy as jnp
from jax import lax
from jax.experimental import pallas as pl
from jax.experimental.pallas import tpu as pltpu
from jax.sharding import PartitionSpec as P

STEP = 20
MESH = pl.DeviceIdType.MESH


def relay_kernel(
    down_hidden, up_hidden, down_cot, up_cot, down_weight, up_weight,
    totals, down_values, up_values,
    raw, normed, feats, cots, weights, grad_out, grad_in, part_out, part_in,
    load_sem, relay_send, relay_recv, cot_send, cot_recv, pass_recv, side_send, right_recv, left_recv,
    part_send, part_recv, grad_send, grad_recv,
):
    sections, dp, tensor = (lax.axis_size(a) for a in ("section", "dp", "tensor"))
    s, d, t = (lax.axis_index(a) for a in ("section", "dp", "tensor"))
    rows = raw.shape[2]
    groups = 4
    blocks = feats.shape[4]
    onward = (lax.rem(s + 1, sections), lax.rem(s + sections - 1, sections))
    right, left = lax.rem(t + 1, tensor), lax.rem(t + tensor - 1, tensor)
    mirror = sections - 1 - s
    sibling = d + 1 - 2 * lax.rem(d, 2)

    def kind_of(offset):
        kind = lax.rem(t + offset + 4, 4)
        return lax.rem(kind, 2), lax.div(kind, 2)

    half, pair = kind_of(0)
    other = 1 - half

    barrier = pltpu.get_barrier_semaphore()
    for way in range(2):
        for peer in range(dp):
            pl.semaphore_signal(barrier, device_id={"section": onward[way], "dp": peer}, device_id_type=MESH)
    for step in range(1, dp):
        pl.semaphore_signal(barrier, device_id={"dp": lax.rem(d + step, dp)}, device_id_type=MESH)
    pl.semaphore_signal(barrier, device_id={"tensor": right}, device_id_type=MESH)
    pl.semaphore_signal(barrier, device_id={"tensor": left}, device_id_type=MESH)
    pl.semaphore_signal(barrier, device_id={"section": mirror}, device_id_type=MESH)

    loads = []
    for way, source in enumerate((down_hidden, up_hidden)):
        for j in range(2):
            loads.append(pltpu.make_async_copy(source.at[2 * j + pair], raw.at[way, j], load_sem.at[2 * way + j]))
    for way, source in enumerate((down_cot, up_cot)):
        loads.append(pltpu.make_async_copy(source, cots.at[way, :, d], load_sem.at[4 + way]))
    for way, source in enumerate((down_weight, up_weight)):
        loads.append(pltpu.make_async_copy(source.at[d], weights.at[way], load_sem.at[6 + way]))
    for load in loads:
        load.start()

    def normalize(way):
        loads[2 * way].wait()
        loads[2 * way + 1].wait()
        for j in range(2):
            values = raw[way, j].astype(jnp.float32)
            factor = lax.rsqrt(jnp.mean(values * values, axis=-1, keepdims=True) + 1e-05)
            for peer in range(dp):
                for block in range(blocks):
                    at = pl.multiple_of(((peer * 2 + half) * blocks + block) * 128, 128)
                    chosen = raw[way, j, :, pl.ds(at, 128)].astype(jnp.float32)
                    normed[way, peer, j, block] = (chosen * factor).astype(jnp.bfloat16)

    def relay(way):
        for peer in range(dp):
            pltpu.make_async_remote_copy(
                src_ref=normed.at[way, peer],
                dst_ref=feats.at[way, half, pair, :, :, d],
                send_sem=relay_send,
                recv_sem=relay_recv.at[way],
                device_id={"section": onward[way], "dp": peer},
                device_id_type=MESH,
            ).start()

    def share_cots():
        loads[4].wait()
        loads[5].wait()
        piece = cots.at[:, :, d]
        for step in range(2, dp, 2):
            pltpu.make_async_remote_copy(
                src_ref=piece,
                dst_ref=piece,
                send_sem=cot_send,
                recv_sem=cot_recv,
                device_id={"dp": lax.rem(d + step, dp)},
                device_id_type=MESH,
            ).start()
        pass_cots(d)

    def pass_cots(owner):
        piece = cots.at[:, :, owner]
        pltpu.make_async_remote_copy(
            src_ref=piece,
            dst_ref=piece,
            send_sem=cot_send,
            recv_sem=pass_recv,
            device_id={"dp": sibling},
            device_id_type=MESH,
        ).start()

    def side(way, step, rightward):
        j = (0 if rightward else 1) if step != 1 else (1 if rightward else 0)
        h, p = kind_of(0 if step < 2 else (-1 if rightward else 1))
        piece = feats.at[way, h, p, j]
        return pltpu.make_async_remote_copy(
            src_ref=piece,
            dst_ref=piece,
            send_sem=side_send.at[way],
            recv_sem=(right_recv if rightward else left_recv).at[way, step],
            device_id={"tensor": right if rightward else left},
            device_id_type=MESH,
        )

    def side_wait(way, step):
        for rightward in (True, False):
            piece = feats.at[way, 0, 0, 0]
            pltpu.make_async_copy(piece, piece, (right_recv if rightward else left_recv).at[way, step]).wait()

    def mirrored(way, which):
        return pltpu.make_async_remote_copy(
            src_ref=grad_out.at[way, which],
            dst_ref=grad_in.at[way, which],
            send_sem=grad_send.at[way, which],
            recv_sem=grad_recv.at[way, which],
            device_id={"section": mirror},
            device_id_type=MESH,
        )

    order = [(p, j) for p in range(2) for j in range(2)]

    def gradient(way, which, position):
        features = jnp.concatenate(
            [
                jnp.concatenate([feats[way, position, p, j, block].reshape(-1, 128) for p, j in order], axis=0)
                for block in range(blocks)
            ],
            axis=1,
        )
        cot = jnp.concatenate([cots[way, 2 * j + p].reshape(-1, 128) for p, j in order], axis=0)
        grad = lax.dot_general(features, cot, (((0,), (0,)), ((), ())), preferred_element_type=jnp.float32)
        totals[way, position] = grad
        grad_out[way, which] = grad.astype(jnp.bfloat16)
        mirrored(way, which).start()

    def project(way, which):
        p = pair if which == 0 else 1 - pair
        for j in range(2):
            features = jnp.concatenate(
                [feats[way, h, p, j, block].reshape(-1, 128) for h in range(2) for block in range(blocks)], axis=1
            )
            part = jnp.dot(features, weights[way], preferred_element_type=jnp.float32)
            part_out[way, which, :, j] = part.astype(jnp.bfloat16).reshape(dp, rows, 128)
        for step in range(1, dp):
            peer = lax.rem(d + step, dp)
            pltpu.make_async_remote_copy(
                src_ref=part_out.at[way, which, peer],
                dst_ref=part_in.at[way, which, step - 1],
                send_sem=part_send,
                recv_sem=part_recv.at[way, which],
                device_id={"dp": peer},
                device_id_type=MESH,
            ).start()

    normalize(0)
    pl.semaphore_wait(barrier, 2 * dp + dp - 1 + 3)
    relay(0)
    normalize(1)
    relay(1)
    share_cots()
    loads[6].wait()
    loads[7].wait()
    for way in range(2):
        landed = feats.at[way, 0, 0]
        pltpu.make_async_copy(landed, landed, relay_recv.at[way]).wait()
        for step in range(2):
            for rightward in (True, False):
                side(way, step, rightward).start()
    got = cots.at[:, :, pl.ds(0, dp // 2 - 1)]
    pltpu.make_async_copy(got, got, cot_recv).wait()
    for step in range(2, dp, 2):
        pass_cots(lax.rem(d + step, dp))
    for way in range(2):
        side_wait(way, 0)
        for rightward in (True, False):
            side(way, 2, rightward).start()
        side_wait(way, 1)
        if way == 0:
            got = cots.at[:, :, pl.ds(0, dp // 2)]
            pltpu.make_async_copy(got, got, pass_recv).wait()
        gradient(way, 0, other)
    for way in range(2):
        project(way, 0)
    for way in range(2):
        side_wait(way, 2)
        gradient(way, 1, half)
    for way in range(2):
        project(way, 1)

    for which, position in ((0, other), (1, half)):
        for way in range(2):
            mirrored(way, which).wait_recv()
            totals[1 - way, position] += grad_in[way, which].astype(jnp.float32)
    for way in range(2):
        for which in range(2):
            got = part_in.at[way, which]
            pltpu.make_async_copy(got, got, part_recv.at[way, which]).wait()
            total = part_out[way, which, d].astype(jnp.float32)
            for step in range(dp - 1):
                total += part_in[way, which, step].astype(jnp.float32)
            total = total.astype(jnp.bfloat16)
            for j in range(2):
                (down_values, up_values)[way][2 * j + (pair if which == 0 else 1 - pair)] = total[j]

    pltpu.make_async_copy(normed, normed, relay_send).wait()
    sent = cots.at[:, :, pl.ds(0, dp - 1)]
    pltpu.make_async_copy(sent, sent, cot_send).wait()
    for way in range(2):
        sent = feats.at[way, :, :, :, :, pl.ds(0, dp * 3 // 4)]
        pltpu.make_async_copy(sent, sent, side_send.at[way]).wait()
    pltpu.make_async_copy(part_in, part_in, part_send).wait()
    for way in range(2):
        for which in range(2):
            mirrored(way, which).wait_send()


def shards(
    down_hidden, up_hidden, down_cot, up_cot, down_weight, up_weight, master, moment1, moment2
):
    sections, dp, tensor = (lax.axis_size(a) for a in ("section", "dp", "tensor"))
    tokens, width = down_hidden.shape[1:]
    groups = 4
    rows = tokens // groups
    shard = width // dp
    blocks = shard // 2 // 128
    hbm = pl.BlockSpec(memory_space=pltpu.HBM)
    vmem = pl.BlockSpec(memory_space=pltpu.VMEM)
    bf16, f32 = jnp.bfloat16, jnp.float32
    DMA = pltpu.SemaphoreType.DMA
    totals, down_values, up_values = pl.pallas_call(
        relay_kernel,
        out_shape=(
            jax.ShapeDtypeStruct((2, 2, blocks * 128, 128), f32),
            jax.ShapeDtypeStruct((groups, rows, 128), bf16),
            jax.ShapeDtypeStruct((groups, rows, 128), bf16),
        ),
        in_specs=[hbm] * 6,
        out_specs=(vmem, vmem, vmem),
        scratch_shapes=[
            pltpu.VMEM((2, 2, rows, width), bf16),
            pltpu.VMEM((2, dp, 2, blocks, rows, 128), bf16),
            pltpu.VMEM((2, 2, 2, 2, blocks, dp, rows, 128), bf16),
            pltpu.VMEM((2, groups, dp, rows, 128), bf16),
            pltpu.VMEM((2, shard, 128), bf16),
            pltpu.VMEM((2, 2, blocks * 128, 128), bf16),
            pltpu.VMEM((2, 2, blocks * 128, 128), bf16),
            pltpu.VMEM((2, 2, dp, 2, rows, 128), bf16),
            pltpu.VMEM((2, 2, dp - 1, 2, rows, 128), bf16),
            DMA((8,)),
            DMA,
            DMA((2,)),
            DMA,
            DMA,
            DMA,
            DMA((2,)),
            DMA((2, 3)),
            DMA((2, 3)),
            DMA,
            DMA((2, 2)),
            DMA((2, 2)),
            DMA((2, 2)),
        ],
        compiler_params=pltpu.CompilerParams(
            collective_id=0, has_side_effects=True, vmem_limit_bytes=60 * 1024 * 1024
        ),
    )(
        down_hidden.reshape(groups, rows, width),
        up_hidden.reshape(groups, rows, width),
        down_cot.reshape(groups, rows, 128),
        up_cot.reshape(groups, rows, 128),
        down_weight.reshape(dp, shard, 128),
        up_weight.reshape(dp, shard, 128),
    )
    totals = totals.reshape(master.shape)
    new_moment1 = 0.9 * moment1 + 0.1 * totals
    new_moment2 = 0.95 * moment2 + 0.05 * totals * totals
    first_fix = 1.0 - 0.9**STEP
    second_fix = 1.0 - 0.95**STEP
    new_master = master - 0.05 * (new_moment1 / first_fix) / (
        jnp.sqrt(new_moment2 / second_fix) + 1e-08
    )
    return (
        down_values.reshape(down_cot.shape),
        up_values.reshape(up_cot.shape),
        new_master,
        new_moment1,
        new_moment2,
    )


def solution(mesh):
    return jax.shard_map(
        shards,
        mesh=mesh,
        in_specs=(
            P("section", "dp", None),
            P("section", "dp", None),
            P("section", "dp", "tensor"),
            P("section", "dp", "tensor"),
            P("section", None, "tensor"),
            P("section", None, "tensor"),
            P("section", None, "dp", "tensor"),
            P("section", None, "dp", "tensor"),
            P("section", None, "dp", "tensor"),
        ),
        out_specs=(
            P("section", "dp", "tensor"),
            P("section", "dp", "tensor"),
            P("section", None, "dp", "tensor"),
            P("section", None, "dp", "tensor"),
            P("section", None, "dp", "tensor"),
        ),
        check_vma=False,
    )
```

```python
import functools
import jax
import jax.numpy as jnp
from jax import lax
from jax.experimental import pallas as pl
from jax.experimental.pallas import tpu as pltpu
from jax.sharding import PartitionSpec as P

STEP = 20
MESH = pl.DeviceIdType.MESH


def relay_kernel(
    down_hidden, up_hidden, down_cot, up_cot, down_weight, up_weight,
    totals, down_values, up_values,
    raw, normed, feats, cots, weights, grad_out, grad_in, part_out, part_in,
    load_sem, relay_send, relay_recv, cot_send, cot_recv, pass_recv, side_send, right_recv, left_recv,
    part_send, part_recv, grad_send, grad_recv,
):
    sections, dp, tensor = (lax.axis_size(a) for a in ("section", "dp", "tensor"))
    s, d, t = (lax.axis_index(a) for a in ("section", "dp", "tensor"))
    rows = raw.shape[2]
    groups = 4
    blocks = feats.shape[5]
    onward = (lax.rem(s + 1, sections), lax.rem(s + sections - 1, sections))
    right, left = lax.rem(t + 1, tensor), lax.rem(t + tensor - 1, tensor)
    mirror = sections - 1 - s
    sibling = d + 1 - 2 * lax.rem(d, 2)

    def kind_of(offset):
        kind = lax.rem(t + offset + 4, 4)
        return lax.rem(kind, 2), lax.div(kind, 2)

    half, pair = kind_of(0)
    other = 1 - half

    barrier = pltpu.get_barrier_semaphore()
    for way in range(2):
        for peer in range(dp):
            pl.semaphore_signal(barrier, device_id={"section": onward[way], "dp": peer}, device_id_type=MESH)
    for step in range(1, dp):
        pl.semaphore_signal(barrier, device_id={"dp": lax.rem(d + step, dp)}, device_id_type=MESH)
    pl.semaphore_signal(barrier, device_id={"tensor": right}, device_id_type=MESH)
    pl.semaphore_signal(barrier, device_id={"tensor": left}, device_id_type=MESH)
    pl.semaphore_signal(barrier, device_id={"section": mirror}, device_id_type=MESH)

    loads = []
    for way, source in enumerate((down_hidden, up_hidden)):
        for j in range(2):
            loads.append(pltpu.make_async_copy(source.at[2 * j + pair], raw.at[way, j], load_sem.at[2 * way + j]))
    for way, source in enumerate((down_cot, up_cot)):
        loads.append(pltpu.make_async_copy(source, cots.at[d, way], load_sem.at[4 + way]))
    for way, source in enumerate((down_weight, up_weight)):
        loads.append(pltpu.make_async_copy(source.at[d], weights.at[way], load_sem.at[6 + way]))
    for load in loads:
        load.start()

    def normalize(way):
        loads[2 * way].wait()
        loads[2 * way + 1].wait()
        for j in range(2):
            values = raw[way, j].astype(jnp.float32)
            factor = lax.rsqrt(jnp.mean(values * values, axis=-1, keepdims=True) + 1e-05)
            for peer in range(dp):
                for block in range(blocks):
                    at = pl.multiple_of(((peer * 2 + half) * blocks + block) * 128, 128)
                    chosen = raw[way, j, :, pl.ds(at, 128)].astype(jnp.float32)
                    normed[way, peer, j, block] = (chosen * factor).astype(jnp.bfloat16)

    def relay(way):
        for peer in range(dp):
            pltpu.make_async_remote_copy(
                src_ref=normed.at[way, peer],
                dst_ref=feats.at[way, half, pair, d],
                send_sem=relay_send,
                recv_sem=relay_recv.at[way],
                device_id={"section": onward[way], "dp": peer},
                device_id_type=MESH,
            ).start()

    def share_cots():
        loads[4].wait()
        loads[5].wait()
        piece = cots.at[d]
        for step in range(2, dp, 2):
            pltpu.make_async_remote_copy(
                src_ref=piece,
                dst_ref=piece,
                send_sem=cot_send,
                recv_sem=cot_recv,
                device_id={"dp": lax.rem(d + step, dp)},
                device_id_type=MESH,
            ).start()
        pass_cots(d)

    def pass_cots(owner):
        piece = cots.at[owner]
        pltpu.make_async_remote_copy(
            src_ref=piece,
            dst_ref=piece,
            send_sem=cot_send,
            recv_sem=pass_recv,
            device_id={"dp": sibling},
            device_id_type=MESH,
        ).start()

    def side(way, step, rightward):
        part = (0 if rightward else 1) if step != 1 else (1 if rightward else 0)
        h, p = kind_of(0 if step < 2 else (-1 if rightward else 1))
        piece = feats.at[way, h, p, pl.ds(part * (dp // 2), dp // 2)]
        return pltpu.make_async_remote_copy(
            src_ref=piece,
            dst_ref=piece,
            send_sem=side_send.at[way],
            recv_sem=(right_recv if rightward else left_recv).at[way, step],
            device_id={"tensor": right if rightward else left},
            device_id_type=MESH,
        )

    def side_wait(way, step):
        for rightward in (True, False):
            piece = feats.at[way, 0, 0, pl.ds(0, dp // 2)]
            pltpu.make_async_copy(piece, piece, (right_recv if rightward else left_recv).at[way, step]).wait()

    def mirrored(way, which):
        return pltpu.make_async_remote_copy(
            src_ref=grad_out.at[way, which],
            dst_ref=grad_in.at[way, which],
            send_sem=grad_send.at[way, which],
            recv_sem=grad_recv.at[way, which],
            device_id={"section": mirror},
            device_id_type=MESH,
        )

    order = [(p, j) for p in range(2) for j in range(2)]

    def gradient(way, which, position):
        features = jnp.concatenate(
            [
                jnp.concatenate([feats[way, position, p, :, j, block].reshape(-1, 128) for p, j in order], axis=0)
                for block in range(blocks)
            ],
            axis=1,
        )
        cot = jnp.concatenate([cots[:, way, 2 * j + p].reshape(-1, 128) for p, j in order], axis=0)
        grad = lax.dot_general(features, cot, (((0,), (0,)), ((), ())), preferred_element_type=jnp.float32)
        totals[way, position] = grad
        grad_out[way, which] = grad.astype(jnp.bfloat16)
        mirrored(way, which).start()

    def project(way, which):
        p = pair if which == 0 else 1 - pair
        for j in range(2):
            features = jnp.concatenate(
                [feats[way, h, p, :, j, block].reshape(-1, 128) for h in range(2) for block in range(blocks)], axis=1
            )
            part = jnp.dot(features, weights[way], preferred_element_type=jnp.float32)
            part_out[way, which, :, j] = part.astype(jnp.bfloat16).reshape(dp, rows, 128)
        for step in range(1, dp):
            peer = lax.rem(d + step, dp)
            pltpu.make_async_remote_copy(
                src_ref=part_out.at[way, which, peer],
                dst_ref=part_in.at[way, which, step - 1],
                send_sem=part_send,
                recv_sem=part_recv.at[way, which],
                device_id={"dp": peer},
                device_id_type=MESH,
            ).start()

    normalize(0)
    pl.semaphore_wait(barrier, 2 * dp + dp - 1 + 3)
    relay(0)
    normalize(1)
    relay(1)
    share_cots()
    loads[6].wait()
    loads[7].wait()
    for way in range(2):
        landed = feats.at[way, 0, 0]
        pltpu.make_async_copy(landed, landed, relay_recv.at[way]).wait()
        for step in range(2):
            for rightward in (True, False):
                side(way, step, rightward).start()
    got = cots.at[pl.ds(0, dp // 2 - 1)]
    pltpu.make_async_copy(got, got, cot_recv).wait()
    for step in range(2, dp, 2):
        pass_cots(lax.rem(d + step, dp))
    for way in range(2):
        side_wait(way, 0)
        for rightward in (True, False):
            side(way, 2, rightward).start()
        side_wait(way, 1)
        if way == 0:
            got = cots.at[pl.ds(0, dp // 2)]
            pltpu.make_async_copy(got, got, pass_recv).wait()
        gradient(way, 0, other)
    for way in range(2):
        project(way, 0)
    for way in range(2):
        side_wait(way, 2)
        gradient(way, 1, half)
    for way in range(2):
        project(way, 1)

    for which, position in ((0, other), (1, half)):
        for way in range(2):
            mirrored(way, which).wait_recv()
            totals[1 - way, position] += grad_in[way, which].astype(jnp.float32)
    for way in range(2):
        for which in range(2):
            got = part_in.at[way, which]
            pltpu.make_async_copy(got, got, part_recv.at[way, which]).wait()
            total = part_out[way, which, d].astype(jnp.float32)
            for step in range(dp - 1):
                total += part_in[way, which, step].astype(jnp.float32)
            total = total.astype(jnp.bfloat16)
            for j in range(2):
                (down_values, up_values)[way][2 * j + (pair if which == 0 else 1 - pair)] = total[j]

    pltpu.make_async_copy(normed, normed, relay_send).wait()
    sent = cots.at[pl.ds(0, dp - 1)]
    pltpu.make_async_copy(sent, sent, cot_send).wait()
    for way in range(2):
        sent = feats.at[way, :, :, pl.ds(0, dp * 3 // 4)]
        pltpu.make_async_copy(sent, sent, side_send.at[way]).wait()
    pltpu.make_async_copy(part_in, part_in, part_send).wait()
    for way in range(2):
        for which in range(2):
            mirrored(way, which).wait_send()


def adam_kernel(
    down_values, up_values, totals, master, moment1, moment2,
    down_out, up_out, new_master, new_moment1, new_moment2, held, value_sem, held_sem,
):
    moves = [
        pltpu.make_async_copy(down_values, down_out, value_sem.at[0]),
        pltpu.make_async_copy(up_values, up_out, value_sem.at[1]),
    ]
    for move in moves:
        move.start()
    first_fix = 1.0 - 0.9**STEP
    second_fix = 1.0 - 0.95**STEP
    for replica in range(2):
        for part in range(totals.shape[1]):
            total = totals[replica, part]
            first = 0.9 * moment1[replica, part] + 0.1 * total
            second = 0.95 * moment2[replica, part] + 0.05 * total * total
            held[0, replica, part] = master[replica, part] - 0.05 * (first / first_fix) / (
                jnp.sqrt(second / second_fix) + 1e-08
            )
            held[1, replica, part] = first
            held[2, replica, part] = second
            for index, target in enumerate((new_master, new_moment1, new_moment2)):
                move = pltpu.make_async_copy(
                    held.at[index, replica, part], target.at[replica, part], held_sem.at[index, replica, part]
                )
                move.start()
                moves.append(move)
    for move in moves:
        move.wait()


def shards(
    down_hidden, up_hidden, down_cot, up_cot, down_weight, up_weight, master, moment1, moment2
):
    sections, dp, tensor = (lax.axis_size(a) for a in ("section", "dp", "tensor"))
    tokens, width = down_hidden.shape[1:]
    groups = 4
    rows = tokens // groups
    shard = width // dp
    blocks = shard // 2 // 128
    hbm = pl.BlockSpec(memory_space=pltpu.HBM)
    vmem = pl.BlockSpec(memory_space=pltpu.VMEM)
    bf16, f32 = jnp.bfloat16, jnp.float32
    DMA = pltpu.SemaphoreType.DMA
    totals, down_values, up_values = pl.pallas_call(
        relay_kernel,
        out_shape=(
            pltpu.VMEM((2, 2, blocks * 128, 128), f32),
            pltpu.VMEM((groups, rows, 128), bf16),
            pltpu.VMEM((groups, rows, 128), bf16),
        ),
        in_specs=[hbm] * 6,
        out_specs=(vmem, vmem, vmem),
        scratch_shapes=[
            pltpu.VMEM((2, 2, rows, width), bf16),
            pltpu.VMEM((2, dp, 2, blocks, rows, 128), bf16),
            pltpu.VMEM((2, 2, 2, dp, 2, blocks, rows, 128), bf16),
            pltpu.VMEM((dp, 2, groups, rows, 128), bf16),
            pltpu.VMEM((2, shard, 128), bf16),
            pltpu.VMEM((2, 2, blocks * 128, 128), bf16),
            pltpu.VMEM((2, 2, blocks * 128, 128), bf16),
            pltpu.VMEM((2, 2, dp, 2, rows, 128), bf16),
            pltpu.VMEM((2, 2, dp - 1, 2, rows, 128), bf16),
            DMA((8,)),
            DMA,
            DMA((2,)),
            DMA,
            DMA,
            DMA,
            DMA((2,)),
            DMA((2, 3)),
            DMA((2, 3)),
            DMA,
            DMA((2, 2)),
            DMA((2, 2)),
            DMA((2, 2)),
        ],
        compiler_params=pltpu.CompilerParams(
            collective_id=0, has_side_effects=True, vmem_limit_bytes=60 * 1024 * 1024
        ),
    )(
        down_hidden.reshape(groups, rows, width),
        up_hidden.reshape(groups, rows, width),
        down_cot.reshape(groups, rows, 128),
        up_cot.reshape(groups, rows, 128),
        down_weight.reshape(dp, shard, 128),
        up_weight.reshape(dp, shard, 128),
    )
    state = totals.shape
    results = pl.pallas_call(
        adam_kernel,
        out_shape=(
            jax.ShapeDtypeStruct(down_values.shape, bf16),
            jax.ShapeDtypeStruct(up_values.shape, bf16),
            jax.ShapeDtypeStruct(state, f32),
            jax.ShapeDtypeStruct(state, f32),
            jax.ShapeDtypeStruct(state, f32),
        ),
        in_specs=[hbm, hbm, vmem, vmem, vmem, vmem],
        out_specs=(hbm,) * 5,
        scratch_shapes=[pltpu.VMEM((3,) + state, f32), DMA((2,)), DMA((3,) + state[:2])],
        compiler_params=pltpu.CompilerParams(vmem_limit_bytes=8 * 1024 * 1024),
    )(down_values, up_values, totals, master.reshape(state), moment1.reshape(state), moment2.reshape(state))
    return (
        results[0].reshape(down_cot.shape),
        results[1].reshape(up_cot.shape),
        results[2].reshape(master.shape),
        results[3].reshape(master.shape),
        results[4].reshape(master.shape),
    )


def solution(mesh):
    return jax.shard_map(
        shards,
        mesh=mesh,
        in_specs=(
            P("section", "dp", None),
            P("section", "dp", None),
            P("section", "dp", "tensor"),
            P("section", "dp", "tensor"),
            P("section", None, "tensor"),
            P("section", None, "tensor"),
            P("section", None, "dp", "tensor"),
            P("section", None, "dp", "tensor"),
            P("section", None, "dp", "tensor"),
        ),
        out_specs=(
            P("section", "dp", "tensor"),
            P("section", "dp", "tensor"),
            P("section", None, "dp", "tensor"),
            P("section", None, "dp", "tensor"),
            P("section", None, "dp", "tensor"),
        ),
        check_vma=False,
    )
```

```python
import functools
import jax
import jax.numpy as jnp
from jax import lax
from jax.experimental import pallas as pl
from jax.experimental.pallas import tpu as pltpu
from jax.sharding import PartitionSpec as P

STEP = 20
MESH = pl.DeviceIdType.MESH


def relay_kernel(
    down_hidden, up_hidden, down_cot, up_cot, down_weight, up_weight,
    totals, down_values, up_values,
    raw, normed, feats, cots, weights, grad_out, grad_in, part_out, part_in,
    load_sem, relay_send, relay_recv, cot_send, cot_recv, pass_recv, side_send, right_recv, left_recv,
    part_send, part_recv, grad_send, grad_recv,
):
    sections, dp, tensor = (lax.axis_size(a) for a in ("section", "dp", "tensor"))
    s, d, t = (lax.axis_index(a) for a in ("section", "dp", "tensor"))
    rows = raw.shape[2]
    groups = 4
    blocks = feats.shape[5]
    onward = (lax.rem(s + 1, sections), lax.rem(s + sections - 1, sections))
    right, left = lax.rem(t + 1, tensor), lax.rem(t + tensor - 1, tensor)
    mirror = sections - 1 - s
    sibling = d + 1 - 2 * lax.rem(d, 2)

    def kind_of(offset):
        kind = lax.rem(t + offset + 4, 4)
        return lax.rem(kind, 2), lax.div(kind, 2)

    half, pair = kind_of(0)
    other = 1 - half

    barrier = pltpu.get_barrier_semaphore()
    for way in range(2):
        for peer in range(dp):
            pl.semaphore_signal(barrier, device_id={"section": onward[way], "dp": peer}, device_id_type=MESH)
    for step in range(1, dp):
        pl.semaphore_signal(barrier, device_id={"dp": lax.rem(d + step, dp)}, device_id_type=MESH)
    pl.semaphore_signal(barrier, device_id={"tensor": right}, device_id_type=MESH)
    pl.semaphore_signal(barrier, device_id={"tensor": left}, device_id_type=MESH)
    pl.semaphore_signal(barrier, device_id={"section": mirror}, device_id_type=MESH)

    loads = []
    for way, source in enumerate((down_hidden, up_hidden)):
        for j in range(2):
            loads.append(pltpu.make_async_copy(source.at[2 * j + pair], raw.at[way, j], load_sem.at[2 * way + j]))
    for way, source in enumerate((down_cot, up_cot)):
        loads.append(pltpu.make_async_copy(source, cots.at[d, way], load_sem.at[4 + way]))
    for way, source in enumerate((down_weight, up_weight)):
        loads.append(pltpu.make_async_copy(source.at[d], weights.at[way], load_sem.at[6 + way]))
    for load in loads:
        load.start()

    def normalize(way):
        loads[2 * way].wait()
        loads[2 * way + 1].wait()
        for j in range(2):
            values = raw[way, j].astype(jnp.float32)
            factor = lax.rsqrt(jnp.mean(values * values, axis=-1, keepdims=True) + 1e-05)
            for peer in range(dp):
                for block in range(blocks):
                    at = pl.multiple_of(((peer * 2 + half) * blocks + block) * 128, 128)
                    chosen = raw[way, j, :, pl.ds(at, 128)].astype(jnp.float32)
                    normed[way, peer, j, block] = (chosen * factor).astype(jnp.bfloat16)

    def relay(way):
        for step in [(k + dp // 2) % dp for k in range(dp)]:
            peer = lax.rem(d + step, dp)
            pltpu.make_async_remote_copy(
                src_ref=normed.at[way, peer],
                dst_ref=feats.at[way, half, pair, d],
                send_sem=relay_send,
                recv_sem=relay_recv.at[way],
                device_id={"section": onward[way], "dp": peer},
                device_id_type=MESH,
            ).start()

    def share_cots():
        loads[4].wait()
        loads[5].wait()
        piece = cots.at[d]
        for step in range(2, dp, 2):
            pltpu.make_async_remote_copy(
                src_ref=piece,
                dst_ref=piece,
                send_sem=cot_send,
                recv_sem=cot_recv,
                device_id={"dp": lax.rem(d + step, dp)},
                device_id_type=MESH,
            ).start()
        pass_cots(d)

    def pass_cots(owner):
        piece = cots.at[owner]
        pltpu.make_async_remote_copy(
            src_ref=piece,
            dst_ref=piece,
            send_sem=cot_send,
            recv_sem=pass_recv,
            device_id={"dp": sibling},
            device_id_type=MESH,
        ).start()

    def side(way, step, rightward):
        part = (0 if rightward else 1) if step != 1 else (1 if rightward else 0)
        h, p = kind_of(0 if step < 2 else (-1 if rightward else 1))
        piece = feats.at[way, h, p, pl.ds(part * (dp // 2), dp // 2)]
        return pltpu.make_async_remote_copy(
            src_ref=piece,
            dst_ref=piece,
            send_sem=side_send.at[way],
            recv_sem=(right_recv if rightward else left_recv).at[way, step],
            device_id={"tensor": right if rightward else left},
            device_id_type=MESH,
        )

    def side_wait(way, step):
        for rightward in (True, False):
            piece = feats.at[way, 0, 0, pl.ds(0, dp // 2)]
            pltpu.make_async_copy(piece, piece, (right_recv if rightward else left_recv).at[way, step]).wait()

    def mirrored(way, which):
        return pltpu.make_async_remote_copy(
            src_ref=grad_out.at[way, which],
            dst_ref=grad_in.at[way, which],
            send_sem=grad_send.at[way, which],
            recv_sem=grad_recv.at[way, which],
            device_id={"section": mirror},
            device_id_type=MESH,
        )

    order = [(p, j) for p in range(2) for j in range(2)]

    def gradient(way, which, position):
        features = jnp.concatenate(
            [
                jnp.concatenate([feats[way, position, p, :, j, block].reshape(-1, 128) for p, j in order], axis=0)
                for block in range(blocks)
            ],
            axis=1,
        )
        cot = jnp.concatenate([cots[:, way, 2 * j + p].reshape(-1, 128) for p, j in order], axis=0)
        grad = lax.dot_general(features, cot, (((0,), (0,)), ((), ())), preferred_element_type=jnp.float32)
        totals[way, position] = grad
        grad_out[way, which] = grad.astype(jnp.bfloat16)
        mirrored(way, which).start()

    def project(way, which):
        p = pair if which == 0 else 1 - pair
        for j in range(2):
            features = jnp.concatenate(
                [feats[way, h, p, :, j, block].reshape(-1, 128) for h in range(2) for block in range(blocks)], axis=1
            )
            part = jnp.dot(features, weights[way], preferred_element_type=jnp.float32)
            part_out[way, which, :, j] = part.astype(jnp.bfloat16).reshape(dp, rows, 128)
        for step in range(1, dp):
            peer = lax.rem(d + step, dp)
            pltpu.make_async_remote_copy(
                src_ref=part_out.at[way, which, peer],
                dst_ref=part_in.at[way, which, step - 1],
                send_sem=part_send,
                recv_sem=part_recv.at[way, which],
                device_id={"dp": peer},
                device_id_type=MESH,
            ).start()

    normalize(0)
    pl.semaphore_wait(barrier, 2 * dp + dp - 1 + 3)
    relay(0)
    normalize(1)
    relay(1)
    share_cots()
    loads[6].wait()
    loads[7].wait()
    for way in range(2):
        landed = feats.at[way, 0, 0]
        pltpu.make_async_copy(landed, landed, relay_recv.at[way]).wait()
        for step in range(2):
            for rightward in (True, False):
                side(way, step, rightward).start()
    got = cots.at[pl.ds(0, dp // 2 - 1)]
    pltpu.make_async_copy(got, got, cot_recv).wait()
    for step in range(2, dp, 2):
        pass_cots(lax.rem(d + step, dp))
    for way in range(2):
        side_wait(way, 0)
        for rightward in (True, False):
            side(way, 2, rightward).start()
        side_wait(way, 1)
        if way == 0:
            got = cots.at[pl.ds(0, dp // 2)]
            pltpu.make_async_copy(got, got, pass_recv).wait()
        gradient(way, 0, other)
    for way in range(2):
        project(way, 0)
    for way in range(2):
        side_wait(way, 2)
        gradient(way, 1, half)
    for way in range(2):
        project(way, 1)

    for which, position in ((0, other), (1, half)):
        for way in range(2):
            mirrored(way, which).wait_recv()
            totals[1 - way, position] += grad_in[way, which].astype(jnp.float32)
    for way in range(2):
        for which in range(2):
            got = part_in.at[way, which]
            pltpu.make_async_copy(got, got, part_recv.at[way, which]).wait()
            total = part_out[way, which, d].astype(jnp.float32)
            for step in range(dp - 1):
                total += part_in[way, which, step].astype(jnp.float32)
            total = total.astype(jnp.bfloat16)
            for j in range(2):
                (down_values, up_values)[way][2 * j + (pair if which == 0 else 1 - pair)] = total[j]

    pltpu.make_async_copy(normed, normed, relay_send).wait()
    sent = cots.at[pl.ds(0, dp - 1)]
    pltpu.make_async_copy(sent, sent, cot_send).wait()
    for way in range(2):
        sent = feats.at[way, :, :, pl.ds(0, dp * 3 // 4)]
        pltpu.make_async_copy(sent, sent, side_send.at[way]).wait()
    pltpu.make_async_copy(part_in, part_in, part_send).wait()
    for way in range(2):
        for which in range(2):
            mirrored(way, which).wait_send()


def adam_kernel(
    down_values, up_values, totals, master, moment1, moment2,
    down_out, up_out, new_master, new_moment1, new_moment2, held, value_sem, held_sem,
):
    moves = [
        pltpu.make_async_copy(down_values, down_out, value_sem.at[0]),
        pltpu.make_async_copy(up_values, up_out, value_sem.at[1]),
    ]
    for move in moves:
        move.start()
    first_fix = 1.0 - 0.9**STEP
    second_fix = 1.0 - 0.95**STEP
    for replica in range(2):
        for part in range(totals.shape[1]):
            total = totals[replica, part]
            first = 0.9 * moment1[replica, part] + 0.1 * total
            second = 0.95 * moment2[replica, part] + 0.05 * total * total
            held[0, replica, part] = master[replica, part] - 0.05 * (first / first_fix) / (
                jnp.sqrt(second / second_fix) + 1e-08
            )
            held[1, replica, part] = first
            held[2, replica, part] = second
            for index, target in enumerate((new_master, new_moment1, new_moment2)):
                move = pltpu.make_async_copy(
                    held.at[index, replica, part], target.at[replica, part], held_sem.at[index, replica, part]
                )
                move.start()
                moves.append(move)
    for move in moves:
        move.wait()


def shards(
    down_hidden, up_hidden, down_cot, up_cot, down_weight, up_weight, master, moment1, moment2
):
    sections, dp, tensor = (lax.axis_size(a) for a in ("section", "dp", "tensor"))
    tokens, width = down_hidden.shape[1:]
    groups = 4
    rows = tokens // groups
    shard = width // dp
    blocks = shard // 2 // 128
    hbm = pl.BlockSpec(memory_space=pltpu.HBM)
    vmem = pl.BlockSpec(memory_space=pltpu.VMEM)
    bf16, f32 = jnp.bfloat16, jnp.float32
    DMA = pltpu.SemaphoreType.DMA
    totals, down_values, up_values = pl.pallas_call(
        relay_kernel,
        out_shape=(
            pltpu.VMEM((2, 2, blocks * 128, 128), f32),
            pltpu.VMEM((groups, rows, 128), bf16),
            pltpu.VMEM((groups, rows, 128), bf16),
        ),
        in_specs=[hbm] * 6,
        out_specs=(vmem, vmem, vmem),
        scratch_shapes=[
            pltpu.VMEM((2, 2, rows, width), bf16),
            pltpu.VMEM((2, dp, 2, blocks, rows, 128), bf16),
            pltpu.VMEM((2, 2, 2, dp, 2, blocks, rows, 128), bf16),
            pltpu.VMEM((dp, 2, groups, rows, 128), bf16),
            pltpu.VMEM((2, shard, 128), bf16),
            pltpu.VMEM((2, 2, blocks * 128, 128), bf16),
            pltpu.VMEM((2, 2, blocks * 128, 128), bf16),
            pltpu.VMEM((2, 2, dp, 2, rows, 128), bf16),
            pltpu.VMEM((2, 2, dp - 1, 2, rows, 128), bf16),
            DMA((8,)),
            DMA,
            DMA((2,)),
            DMA,
            DMA,
            DMA,
            DMA((2,)),
            DMA((2, 3)),
            DMA((2, 3)),
            DMA,
            DMA((2, 2)),
            DMA((2, 2)),
            DMA((2, 2)),
        ],
        compiler_params=pltpu.CompilerParams(
            collective_id=0, has_side_effects=True, vmem_limit_bytes=60 * 1024 * 1024
        ),
    )(
        down_hidden.reshape(groups, rows, width),
        up_hidden.reshape(groups, rows, width),
        down_cot.reshape(groups, rows, 128),
        up_cot.reshape(groups, rows, 128),
        down_weight.reshape(dp, shard, 128),
        up_weight.reshape(dp, shard, 128),
    )
    state = totals.shape
    results = pl.pallas_call(
        adam_kernel,
        out_shape=(
            jax.ShapeDtypeStruct(down_values.shape, bf16),
            jax.ShapeDtypeStruct(up_values.shape, bf16),
            jax.ShapeDtypeStruct(state, f32),
            jax.ShapeDtypeStruct(state, f32),
            jax.ShapeDtypeStruct(state, f32),
        ),
        in_specs=[hbm, hbm, vmem, vmem, vmem, vmem],
        out_specs=(hbm,) * 5,
        scratch_shapes=[pltpu.VMEM((3,) + state, f32), DMA((2,)), DMA((3,) + state[:2])],
        compiler_params=pltpu.CompilerParams(vmem_limit_bytes=8 * 1024 * 1024),
    )(down_values, up_values, totals, master.reshape(state), moment1.reshape(state), moment2.reshape(state))
    return (
        results[0].reshape(down_cot.shape),
        results[1].reshape(up_cot.shape),
        results[2].reshape(master.shape),
        results[3].reshape(master.shape),
        results[4].reshape(master.shape),
    )


def solution(mesh):
    return jax.shard_map(
        shards,
        mesh=mesh,
        in_specs=(
            P("section", "dp", None),
            P("section", "dp", None),
            P("section", "dp", "tensor"),
            P("section", "dp", "tensor"),
            P("section", None, "tensor"),
            P("section", None, "tensor"),
            P("section", None, "dp", "tensor"),
            P("section", None, "dp", "tensor"),
            P("section", None, "dp", "tensor"),
        ),
        out_specs=(
            P("section", "dp", "tensor"),
            P("section", "dp", "tensor"),
            P("section", None, "dp", "tensor"),
            P("section", None, "dp", "tensor"),
            P("section", None, "dp", "tensor"),
        ),
        check_vma=False,
    )
```
